256 devices in a mesh: dp: 16 (over y, x), ctx: 16 (over z, core).
Axes of the slice: x: 4, y: 4, z: 8, core: 2. Of those that a mesh axis runs over, the one named last changes fastest.
Arguments:
- query: bfloat16 [16, 4096, 8, 128], P('dp', 'ctx'), may hold values from -50 to 50
- keys: bfloat16 [16, 4096, 128], P('dp', 'ctx'), may hold values from -5 to 5
- values: bfloat16 [16, 4096, 128], P('dp', 'ctx'), may hold values from -6 to 6
- doc_ids: int32 [16, 4096], P('dp', 'ctx'), may hold values from 0 to 15, never falling along the last dimension, each value on 1 to 2304 neighbouring positions
- grad_out: bfloat16 [16, 4096, 8, 128], P('dp', 'ctx'), may hold values from -6 to 6
- relabel: int32 [1], replicated, may hold values from 1 to 15
Outputs:
- attended: bfloat16 [16, 4096, 8, 128], P('dp', 'ctx')
- grad_query: bfloat16 [16, 4096, 8, 128], P('dp', 'ctx')
- grad_keys: bfloat16 [16, 4096, 128], P('dp', 'ctx')
- grad_values: bfloat16 [16, 4096, 128], P('dp', 'ctx')
The draws below stay inside these ranges and needn't reach their ends.
Inputs may be any that keep to these rules, and one draw needn't show every extreme that they name: `doc_ids`: document numbers never fall along a sequence; each document covers at most 2304 positions and one covers exactly 2304.
All inputs are finite; a program needn't handle non-finite values.
Results may differ from the reference program's by a relative error of at most 0.039.
Values may be sent and summed in bfloat16 or wider, within the bound.
A program may use at most 64 MiB of HBM per device.

```python
import math
import jax
import jax.numpy as jnp
import numpy as np
from jax import lax

TOK_DEV = 256
HEADS = 8
HD = 128
SEQS = 16
TOKENS = 4096
DOC_MAX = 2304
DOCS = 16
N_DP = 16


def shared_keys(key):
    return jax.random.normal(key, (SEQS, TOKENS, HD), jnp.float32)


def draw_keys(key, part):
    base = shared_keys(key)
    return jnp.clip(base, -5.0, 5.0).astype(jnp.bfloat16)


def draw_query(key, part):
    key = jax.random.fold_in(key, 7)
    shape = (SEQS, TOKENS, HEADS, HD)
    return jnp.clip(3.0 * jax.random.normal(key, shape, jnp.float32), -12.0, 12.0).astype(jnp.bfloat16)


def levels(own_key, dims, pieces, least, top_value):
    gain = 1.0
    for axis_at, parts in pieces:
        draws = jax.random.uniform(jax.random.fold_in(jax.random.fold_in(own_key, 6), axis_at), (parts,), jnp.float32, least / len(pieces), top_value / len(pieces))
        gain = gain * jnp.repeat(jnp.exp(draws), dims[axis_at] // parts).reshape((-1,) + (1,) * (len(dims) - 1 - axis_at))
    return gain


def length_profile(number_of, total, reach, lean):
    portions = [(1 << 20) // math.isqrt(grade ** lean) + 1 for grade in range(2, number_of + 1)]
    surplus, given = total - reach - (number_of - 1), [1] * (number_of - 1)
    while surplus > 0:
        movable = [i for i in range(number_of - 1) if given[i] < reach]
        mass, remaining = sum([portions[i] for i in movable]), surplus
        for i in movable:
            addition = min(reach - given[i], max(1, remaining * portions[i] // mass), surplus)
            given[i] = given[i] + addition
            surplus = surplus - addition
    return np.array([reach] + given)


def uneven(stream_key, amount, total, bound, skew):
    if amount == 2:
        one = jax.random.randint(stream_key, (), max(1, total - bound), min(bound, total - 1) + 1)
        return jnp.stack([one, total - one])
    tallies = jnp.asarray(length_profile(amount, total, bound, skew), jnp.int32)
    pairs = (amount - 1) // 2
    giver, sink = tallies[1:1 + 2 * pairs:2], tallies[2:2 + 2 * pairs:2]
    margin = jnp.minimum(giver - 1, bound - sink)
    shifted = jax.random.randint(jax.random.fold_in(stream_key, 1), (pairs,), 0, 1 << 20) % (margin + 1)
    tallies = tallies.at[1:1 + 2 * pairs:2].set(giver - shifted).at[2:2 + 2 * pairs:2].set(sink + shifted)
    return tallies[jax.random.permutation(jax.random.fold_in(stream_key, 2), amount)]


def bell_draw(own_key, dims, spread, bound, cuts=(), kind=jnp.bfloat16):
    loudness = levels(own_key, dims, cuts, -0.22, 0.18) if cuts else 1.0
    drawn = jax.random.normal(own_key, dims, jnp.float32) * spread * loudness
    return jnp.minimum(jnp.maximum(drawn, -bound), bound).astype(kind)


def setup_inputs(seed: int = 0) -> dict:
    streams_of = jax.random.split(jax.random.key(seed), 7)
    query = draw_query(jax.random.fold_in(streams_of[6], 71), 0)
    keys = draw_keys(jax.random.fold_in(streams_of[6], 71), 0)
    values = bell_draw(streams_of[2], (SEQS, TOKENS, HD), 1.0, 6.0, ((0, 16), (1, 16)))
    doc_ids = jax.vmap(lambda own: jnp.searchsorted(jnp.cumsum(uneven(own, DOCS, TOKENS, DOC_MAX, 2)), jnp.arange(TOKENS), side="right"))(jax.random.split(streams_of[3], SEQS)).reshape((SEQS, TOKENS)).astype(jnp.int32)
    grad_out = bell_draw(streams_of[4], (SEQS, TOKENS, HEADS, HD), 1.0, 6.0, ((0, 16), (1, 16)))
    relabel = jax.random.randint(streams_of[5], (1,), 1, N_DP).astype(jnp.int32)
    return dict(query=query, keys=keys, values=values, doc_ids=doc_ids, grad_out=grad_out, relabel=relabel)


def sequence_pass(args):
    query, keys, values, grad_out, docs = args
    scale = HD ** -0.5
    span = DOC_MAX + TOK_DEV
    key_pad = jnp.concatenate([jnp.zeros((DOC_MAX, HD), keys.dtype), keys], axis=0)
    val_pad = jnp.concatenate([jnp.zeros((DOC_MAX, HD), values.dtype), values], axis=0)
    doc_pad = jnp.concatenate([jnp.full((DOC_MAX,), -1, jnp.int32), docs.astype(jnp.int32)], axis=0)

    def block_pass(grads, index):
        key_acc, val_acc = grads
        start = (index * TOK_DEV).astype(jnp.int32)
        q_rows = lax.dynamic_slice_in_dim(query, start, TOK_DEV, 0).reshape(TOK_DEV * HEADS, HD)
        g_rows = lax.dynamic_slice_in_dim(grad_out, start, TOK_DEV, 0).reshape(TOK_DEV * HEADS, HD)
        q_doc = jnp.repeat(lax.dynamic_slice_in_dim(docs.astype(jnp.int32), start, TOK_DEV, 0), HEADS)
        q_pos = jnp.repeat(start + jnp.arange(TOK_DEV, dtype=jnp.int32), HEADS)
        key_win = lax.dynamic_slice_in_dim(key_pad, start, span, 0)
        val_win = lax.dynamic_slice_in_dim(val_pad, start, span, 0)
        doc_win = lax.dynamic_slice_in_dim(doc_pad, start, span, 0)
        key_pos = start - DOC_MAX + jnp.arange(span, dtype=jnp.int32)
        allowed = (q_doc[:, None] == doc_win[None, :]) & (key_pos[None, :] <= q_pos[:, None])
        scores = jnp.dot(q_rows, key_win.T, preferred_element_type=jnp.float32) * scale
        peak = jnp.max(jnp.where(allowed, scores, -jnp.inf), axis=1)
        total = jnp.sum(jnp.where(allowed, jnp.exp(scores - peak[:, None]), 0.0), axis=1)
        log_norm = peak + jnp.log(total)
        probs = jnp.where(allowed, jnp.exp(scores - log_norm[:, None]), 0.0)
        low_probs = probs.astype(jnp.bfloat16)
        attended = jnp.dot(low_probs, val_win, preferred_element_type=jnp.float32).astype(jnp.bfloat16)
        delta = jnp.sum(g_rows.astype(jnp.float32) * attended.astype(jnp.float32), axis=1)
        grad_probs = jnp.dot(g_rows, val_win.T, preferred_element_type=jnp.float32)
        grad_scores = (probs * (grad_probs - delta[:, None]) * scale).astype(jnp.bfloat16)
        query_grad = jnp.dot(grad_scores, key_win, preferred_element_type=jnp.float32).astype(jnp.bfloat16)
        key_term = jnp.dot(grad_scores.T, q_rows, preferred_element_type=jnp.float32)
        val_term = jnp.dot(low_probs.T, g_rows, preferred_element_type=jnp.float32)
        key_acc = lax.dynamic_update_slice_in_dim(key_acc, lax.dynamic_slice_in_dim(key_acc, start, span, 0) + key_term, start, 0)
        val_acc = lax.dynamic_update_slice_in_dim(val_acc, lax.dynamic_slice_in_dim(val_acc, start, span, 0) + val_term, start, 0)
        return (key_acc, val_acc), (attended.reshape(TOK_DEV, HEADS, HD), query_grad.reshape(TOK_DEV, HEADS, HD))

    empty = jnp.zeros((DOC_MAX + TOKENS, HD), jnp.float32)
    grads, outputs = lax.scan(block_pass, (empty, empty), jnp.arange(TOKENS // TOK_DEV, dtype=jnp.int32))
    attended = outputs[0].reshape(TOKENS, HEADS, HD)
    query_grad = outputs[1].reshape(TOKENS, HEADS, HD)
    return attended, query_grad, grads[0][DOC_MAX:].astype(jnp.bfloat16), grads[1][DOC_MAX:].astype(jnp.bfloat16)


def reference(query, keys, values, doc_ids, grad_out, relabel):
    source = jnp.bitwise_xor(jnp.arange(SEQS, dtype=jnp.int32), relabel[0].astype(jnp.int32))
    picked = (jnp.take(query, source, axis=0), jnp.take(keys, source, axis=0), jnp.take(values, source, axis=0),
              jnp.take(grad_out, source, axis=0), jnp.take(doc_ids, source, axis=0))
    attended, grad_query, grad_keys, grad_values = lax.map(sequence_pass, picked)
    return attended, grad_query, grad_keys, grad_values
```

```python
import functools

import jax
import jax.numpy as jnp
from jax import lax
from jax.experimental import pallas as pl
from jax.experimental.pallas import tpu as pltpu
from jax.sharding import PartitionSpec as P

MESH = pl.DeviceIdType.MESH
NT = (((1,), (1,)), ((), ()))
NN = (((1,), (0,)), ((), ()))
f32, bf16 = jnp.float32, jnp.bfloat16
DOC_MAX = 2304
NEG = -1e30
LOG2E = 1.4426950408889634
ROW_TILE = 1024


def dot(a, b, dims=NN):
    return lax.dot_general(a, b, dims, preferred_element_type=f32)


def partner_of(place, offset):
    out = place
    for bit in range(offset.bit_length()):
        if offset >> bit & 1:
            out = out + (1 - 2 * ((place // (1 << bit)) % 2)) * (1 << bit)
    return out


def kernel(offset, heads, steps, q_ref, g_ref, k_ref, v_ref, doc_ref, att_out, dq_out, dk_out, dv_out,
           kw, vw, kt, dcol, docq, s_scr, m_scr, l_scr, lse, delta, ot, dqt, att_v, dq_v, fin, red_in, red_out,
           gs, gr, rs, rr, ws, wr):
    rows_all, width = q_ref.shape
    block = k_ref.shape[0]
    tiles = rows_all // ROW_TILE
    scale = width ** -0.5
    ring = lax.axis_size("ctx")
    dp, me = lax.axis_index("dp"), lax.axis_index("ctx")
    up, down = lax.rem(me + 1, ring), lax.rem(me + ring - 1, ring)
    partner = partner_of(dp, offset)

    barrier = pltpu.get_barrier_semaphore()
    for where in ((dp, up), (dp, down), (partner, me)):
        pl.semaphore_signal(barrier, inc=1, device_id=where, device_id_type=MESH)

    kw[0, 0:block] = k_ref[...]
    docs = doc_ref[...].astype(f32)
    kw[0, block:] = jnp.concatenate(
        [docs[:, 128 * i:128 * i + 128] for i in range(block // 128)] + [jnp.zeros((16 - block // 128, 128), f32)], axis=0
    ).astype(bf16)
    vw[0] = v_ref[...]
    pl.semaphore_wait(barrier, 3)

    def hop(buf, part, d):
        return pltpu.make_async_remote_copy(
            src_ref=buf.at[d], dst_ref=buf.at[d + 1], send_sem=gs.at[part, d], recv_sem=gr.at[part, d + 1],
            device_id=(dp, up), device_id_type=MESH)

    def landed(buf, part, d):
        pltpu.make_async_remote_copy(
            src_ref=buf.at[d], dst_ref=buf.at[d], send_sem=gs.at[part, d], recv_sem=gr.at[part, d],
            device_id=(dp, up), device_id_type=MESH).wait_recv()

    hop(kw, 0, 0).start()
    hop(vw, 1, 0).start()

    def spread(d):
        tail = kw[d, block:].astype(f32)
        for i in range(block // 128):
            col = jnp.broadcast_to(tail[i:i + 1], (128, 128)).T
            dcol[128 * i:128 * i + 128, :] = jnp.where(me >= d, col, -1.0)

    spread(0)
    group = 128 // heads
    pick = (lax.broadcasted_iota(jnp.int32, (group, 128), 1) // heads == lax.broadcasted_iota(jnp.int32, (group, 128), 0)).astype(f32)
    for i in range(rows_all // 128):
        docq[:, 128 * i:128 * i + 128] = jnp.sum(dcol[group * i:group * i + group, :] * pick, axis=0, keepdims=True)

    def lanes_of(t):
        return pl.ds(pl.multiple_of(t * ROW_TILE, ROW_TILE), ROW_TILE)

    def forward(d, own):
        kt[d] = kw[d, 0:block].T
        vt = vw[d].T
        mark = jnp.concatenate([dcol[...]] * (ROW_TILE // 128), axis=1)

        def tile(t, carry):
            lanes = lanes_of(t)
            s = dot(kw[d, 0:block], q_ref[lanes, :], NT) * (scale * LOG2E)
            ok = mark == docq[:, lanes]
            if own:
                token = (lax.broadcasted_iota(jnp.int32, (1, ROW_TILE), 1) + t * ROW_TILE) // heads
                ok = ok & (lax.broadcasted_iota(jnp.int32, (block, ROW_TILE), 0) <= token)
            s = jnp.where(ok, s, NEG)
            s_scr[d, :, lanes] = s
            m = jnp.max(jnp.max(s.reshape(block // 8, 8, ROW_TILE), axis=0), axis=0, keepdims=True)
            if own:
                p = jnp.exp2(s - m)
                l_scr[:, lanes] = jnp.sum(p.reshape(block // 8, 8, ROW_TILE), axis=0)
                ot[:, lanes] = dot(vt, p.astype(bf16))
            else:
                old = m_scr[:, lanes]
                m = jnp.maximum(old, m)
                decay = jnp.exp2(old - m)
                p = jnp.exp2(s - m)
                l_scr[:, lanes] = l_scr[:, lanes] * decay + jnp.sum(p.reshape(block // 8, 8, ROW_TILE), axis=0)
                ot[:, lanes] = ot[:, lanes] * decay + dot(vt, p.astype(bf16))
            m_scr[:, lanes] = m
            return carry

        lax.fori_loop(0, tiles, tile, 0)

    forward(0, True)

    def gather_step(d, carry):
        landed(kw, 0, d)

        @pl.when(d < steps)
        def _():
            hop(kw, 0, d).start()

        landed(vw, 1, d)

        @pl.when(d < steps)
        def _():
            hop(vw, 1, d).start()

        spread(d)
        forward(d, False)
        return carry

    lax.fori_loop(1, steps + 1, gather_step, 0)

    def send_out(src, dst, sem):
        return pltpu.make_async_remote_copy(
            src_ref=src, dst_ref=dst, send_sem=ws.at[sem], recv_sem=wr.at[sem],
            device_id=(partner, me), device_id_type=MESH)

    def att_copy(t):
        return send_out(att_v.at[lanes_of(t)], att_out.at[lanes_of(t)], t)

    def dq_copy(t):
        return send_out(dq_v.at[lanes_of(t)], dq_out.at[lanes_of(t)], tiles + t)

    def finish(t, carry):
        lanes = lanes_of(t)
        total = jnp.sum(l_scr[:, lanes], axis=0, keepdims=True)
        lse[:, lanes] = m_scr[:, lanes] + jnp.log2(total)
        low = (ot[:, lanes] * (1.0 / total)).astype(bf16).astype(f32)
        att_v[lanes, :] = low.T.astype(bf16)
        att_copy(t).start()
        delta[:, lanes] = jnp.sum(low * g_ref[lanes, :].astype(f32).T, axis=0, keepdims=True)
        dqt[:, lanes] = jnp.zeros((width, ROW_TILE), f32)
        return carry

    lax.fori_loop(0, tiles, finish, 0)

    def reduce_hop(part, d):
        return pltpu.make_async_remote_copy(
            src_ref=red_out.at[part, d], dst_ref=red_in.at[part, d - 1], send_sem=rs.at[part, d], recv_sem=rr.at[part, d - 1],
            device_id=(dp, down), device_id_type=MESH)

    def reduce_landed(part, d):
        pltpu.make_async_remote_copy(
            src_ref=red_out.at[part, d], dst_ref=red_in.at[part, d], send_sem=rs.at[part, d], recv_sem=rr.at[part, d],
            device_id=(dp, down), device_id_type=MESH).wait_recv()

    def backward(d):
        def tile(t, carry):
            dk, dv = carry
            lanes = lanes_of(t)
            g, q = g_ref[lanes, :], q_ref[lanes, :]
            p = jnp.exp2(s_scr[d, :, lanes] - lse[:, lanes])
            ds = (p * (dot(vw[d], g, NT) - delta[:, lanes])).astype(bf16)
            dqt[:, lanes] += dot(kt[d], ds)
            return dk + dot(ds, q), dv + dot(p.astype(bf16), g)

        zero = jnp.zeros((block, width), f32)
        return lax.fori_loop(0, tiles, tile, (zero, zero))

    terms = backward(steps)
    for part in range(2):
        red_out[part, steps] = terms[part].astype(bf16)
        reduce_hop(part, steps).start()

    def back_step(n, carry):
        d = steps - n
        terms = backward(d)
        for part in range(2):
            reduce_landed(part, d)
            red_out[part, d] = (terms[part] + red_in[part, d].astype(f32)).astype(bf16)
            reduce_hop(part, d).start()
        return carry

    lax.fori_loop(1, steps, back_step, 0)
    terms = backward(0)

    def finish_dq(t, carry):
        lanes = lanes_of(t)
        dq_v[lanes, :] = (dqt[:, lanes] * scale).T.astype(bf16)
        dq_copy(t).start()
        return carry

    lax.fori_loop(0, tiles, finish_dq, 0)
    ends = []
    for part, (factor, out) in enumerate(((scale, dk_out), (1.0, dv_out))):
        reduce_landed(part, 0)
        fin[part] = ((terms[part] + red_in[part, 0].astype(f32)) * factor).astype(bf16)
        ends.append(send_out(fin.at[part], out, 2 * tiles + part))
        ends[-1].start()

    def drain(d, carry):
        for part, buf in enumerate((kw, vw)):
            hop(buf, part, d).wait_send()
            reduce_hop(part, d + 1).wait_send()
        return carry

    lax.fori_loop(0, steps, drain, 0)

    def drain_out(t, carry):
        att_copy(t).wait()
        dq_copy(t).wait()
        return carry

    lax.fori_loop(0, tiles, drain_out, 0)
    for copy in ends:
        copy.wait()


def attention(offset, heads, q, g, k, v, docs):
    rows, width = q.shape
    block = k.shape[0]
    steps = -(-DOC_MAX // block)
    window = steps + 1
    tiles = rows // ROW_TILE
    vmem, anywhere = pl.BlockSpec(memory_space=pltpu.VMEM), pl.BlockSpec(memory_space=pl.ANY)
    S = jax.ShapeDtypeStruct
    dma = pltpu.SemaphoreType.DMA
    pairs = rows * block * window
    return pl.pallas_call(
        functools.partial(kernel, offset, heads, steps),
        out_shape=(S(q.shape, bf16), S(q.shape, bf16), S(k.shape, bf16), S(k.shape, bf16)),
        in_specs=[vmem] * 5,
        out_specs=[anywhere] * 4,
        scratch_shapes=[
            pltpu.VMEM((window, block + 16, width), bf16),
            pltpu.VMEM((window, block, width), bf16),
            pltpu.VMEM((window, width, block), bf16),
            pltpu.VMEM((block, 128), f32),
            pltpu.VMEM((1, rows), f32),
            pltpu.VMEM((window, block, rows), f32),
            pltpu.VMEM((1, rows), f32),
            pltpu.VMEM((8, rows), f32),
            pltpu.VMEM((1, rows), f32),
            pltpu.VMEM((1, rows), f32),
            pltpu.VMEM((width, rows), f32),
            pltpu.VMEM((width, rows), f32),
            pltpu.VMEM((rows, width), bf16),
            pltpu.VMEM((rows, width), bf16),
            pltpu.VMEM((2, block, width), bf16),
            pltpu.VMEM((2, window, block, width), bf16),
            pltpu.VMEM((2, window, block, width), bf16),
            dma((2, window)), dma((2, window)), dma((2, window)), dma((2, window)),
            dma((2 * tiles + 2,)), dma((2 * tiles + 2,)),
        ],
        compiler_params=pltpu.CompilerParams(collective_id=offset, has_side_effects=True, vmem_limit_bytes=56 * 2**20),
        cost_estimate=pl.CostEstimate(flops=12 * pairs * width, bytes_accessed=8 * rows * width, transcendentals=2 * pairs),
        name=f"attention_{offset}",
    )(q, g, k, v, docs)


def on_device(offsets, query, keys, values, doc_ids, grad_out, relabel):
    _, tokens, heads, width = query.shape
    flat = (query.reshape(tokens * heads, width), grad_out.reshape(tokens * heads, width), keys[0], values[0], doc_ids)
    if len(offsets) == 1:
        outs = attention(offsets[0], heads, *flat)
    else:
        outs = lax.switch(relabel[0] - 1, [functools.partial(attention, offset, heads) for offset in offsets], *flat)
    att, dq, dk, dv = outs
    return att.reshape(query.shape), dq.reshape(query.shape), dk[None], dv[None]


def solution(mesh, offsets=None):
    wide, narrow = P("dp", "ctx", None, None), P("dp", "ctx", None)
    offsets = offsets or tuple(range(1, mesh.shape["dp"]))
    return jax.shard_map(
        functools.partial(on_device, offsets), mesh=mesh,
        in_specs=(wide, narrow, narrow, P("dp", "ctx"), wide, P()),
        out_specs=(wide, wide, narrow, narrow), check_vma=False)
```

```python
import functools

import jax
import jax.numpy as jnp
from jax import lax
from jax.experimental import pallas as pl
from jax.experimental.pallas import tpu as pltpu
from jax.sharding import PartitionSpec as P

MESH = pl.DeviceIdType.MESH
NT = (((1,), (1,)), ((), ()))
NN = (((1,), (0,)), ((), ()))
f32, bf16 = jnp.float32, jnp.bfloat16
DOC_MAX = 2304
NEG = -1e30
LOG2E = 1.4426950408889634
ROW_TILE = 1024
UNROLL = 1


def dot(a, b, dims=NN):
    return lax.dot_general(a, b, dims, preferred_element_type=f32)


def partner_of(place, offset):
    out = place
    for bit in range(offset.bit_length()):
        if offset >> bit & 1:
            out = out + (1 - 2 * ((place // (1 << bit)) % 2)) * (1 << bit)
    return out


def kernel(offset, heads, steps, q_in, g_in, k_in, v_in, doc_in, att_out, dq_out, dk_out, dv_out,
           q_ref, g_ref, doc_v, sums, kv, kt, vt, dcol, docq, s_scr, m_scr, l_scr, lse, delta, ot, dqt, att_v, dq_v, fin, red_in, red_out,
           gs, gr, rs, rr, ws, wr, ls):
    rows_all, width = q_in.shape
    block = k_in.shape[0]
    tiles = rows_all // ROW_TILE
    assert tiles == 2
    scale = width ** -0.5
    ring = lax.axis_size("ctx")
    dp, me = lax.axis_index("dp"), lax.axis_index("ctx")
    up, down = lax.rem(me + 1, ring), lax.rem(me + ring - 1, ring)
    partner = partner_of(dp, offset)

    def load(src, dst, i):
        return pltpu.make_async_copy(src, dst, ls.at[i])

    loads = [load(k_in, kv.at[0, 0, pl.ds(0, block)], 0), load(v_in, kv.at[1, 0, pl.ds(0, block)], 1), load(doc_in, doc_v, 2),
             load(q_in, q_ref, 3), load(g_in, g_ref, 4)]
    for copy in loads:
        copy.start()
    barrier = pltpu.get_barrier_semaphore()
    for where in ((dp, up), (dp, down), (partner, me)):
        pl.semaphore_signal(barrier, inc=1, device_id=where, device_id_type=MESH)
    m_scr[...] = jnp.full_like(m_scr, NEG)
    l_scr[...] = jnp.zeros_like(l_scr)
    ot[...] = jnp.zeros_like(ot)
    dqt[...] = jnp.zeros_like(dqt)
    for part in range(2):
        red_in[part, steps] = jnp.zeros((block, width), bf16)
    loads[2].wait()
    docs = doc_v[...].astype(f32)
    kv[0, 0, block:] = jnp.concatenate(
        [docs[:, 128 * i:128 * i + 128] for i in range(block // 128)] + [jnp.zeros((16 - block // 128, 128), f32)], axis=0
    ).astype(bf16)
    kv[1, 0, block:] = jnp.zeros((16, width), bf16)
    loads[0].wait()
    loads[1].wait()
    pl.semaphore_wait(barrier, 3)

    def hop(part, d):
        return pltpu.make_async_remote_copy(
            src_ref=kv.at[part, d], dst_ref=kv.at[part, d + 1], send_sem=gs.at[part, d], recv_sem=gr.at[part, d + 1],
            device_id=(dp, up), device_id_type=MESH)

    def landed(part, d):
        pltpu.make_async_remote_copy(
            src_ref=kv.at[part, d], dst_ref=kv.at[part, d], send_sem=gs.at[part, d], recv_sem=gr.at[part, d],
            device_id=(dp, up), device_id_type=MESH).wait_recv()

    def gather_relay(part, d):
        @pl.when(d <= steps)
        def _():
            landed(part, d)

        @pl.when(d < steps)
        def _():
            hop(part, d).start()

    hop(0, 0).start()
    hop(1, 0).start()

    def lanes_of(t):
        return pl.ds(pl.multiple_of(t * ROW_TILE, ROW_TILE), ROW_TILE)

    def over_tiles(body, carry):
        return lax.fori_loop(0, tiles, body, carry, unroll=min(UNROLL, tiles))

    def gather_step(d, carry):
        tail = kv[0, d, block:].astype(f32)
        for i in range(block // 128):
            col = jnp.broadcast_to(tail[i:i + 1], (128, 128)).T
            dcol[128 * i:128 * i + 128, :] = jnp.where(me >= d, col, -1.0)

        @pl.when(d == 0)
        def _():
            group = 128 // heads
            pick = (lax.broadcasted_iota(jnp.int32, (group, 128), 1) // heads == lax.broadcasted_iota(jnp.int32, (group, 128), 0)).astype(f32)
            for i in range(rows_all // 128):
                docq[:, 128 * i:128 * i + 128] = jnp.sum(dcol[group * i:group * i + group, :] * pick, axis=0, keepdims=True)
            loads[3].wait()
            loads[4].wait()

        kt[d] = kv[0, d, 0:block].T
        vt[...] = kv[1, d, 0:block].T
        place = lax.broadcasted_iota(jnp.int32, (block, ROW_TILE), 0) - d * block

        def tile(t, carry):
            gather_relay(t, d + 1)
            lanes = lanes_of(t)
            s = dot(kv[0, d, 0:block], q_ref[lanes, :], NT) * (scale * LOG2E)
            mark = jnp.concatenate([dcol[...]] * (ROW_TILE // 128), axis=1)
            token = (lax.broadcasted_iota(jnp.int32, (1, ROW_TILE), 1) + t * ROW_TILE) // heads
            s = jnp.where((mark == docq[:, lanes]) & (place <= token), s, NEG)
            s_scr[d, :, lanes] = s
            old = m_scr[:, lanes]
            m = jnp.max(jnp.max(s.reshape(block // 8, 8, ROW_TILE), axis=0), axis=0, keepdims=True)
            m = jnp.maximum(old, m)
            decay = jnp.exp2(old - m)
            p = jnp.exp2(s - m)
            l_scr[:, lanes] = l_scr[:, lanes] * decay + jnp.sum(p.reshape(block // 8, 8, ROW_TILE), axis=0)
            ot[:, lanes] = ot[:, lanes] * decay + dot(vt[...], p.astype(bf16))
            m_scr[:, lanes] = m
            return carry

        over_tiles(tile, 0)
        return carry

    lax.fori_loop(0, steps + 1, gather_step, 0)

    def send_out(src, dst, sem):
        return pltpu.make_async_remote_copy(
            src_ref=src, dst_ref=dst, send_sem=ws.at[sem], recv_sem=wr.at[sem],
            device_id=(partner, me), device_id_type=MESH)

    def att_copy(t):
        return send_out(att_v.at[lanes_of(t)], att_out.at[lanes_of(t)], t)

    def dq_copy(t):
        return send_out(dq_v.at[lanes_of(t)], dq_out.at[lanes_of(t)], tiles + t)

    def finish(t, carry):
        lanes = lanes_of(t)
        total = jnp.sum(l_scr[:, lanes], axis=0, keepdims=True)
        lse[:, lanes] = m_scr[:, lanes] + jnp.log2(total)
        low = (ot[:, lanes] * (1.0 / total)).astype(bf16).astype(f32)
        att_v[lanes, :] = low.T.astype(bf16)
        att_copy(t).start()
        delta[:, lanes] = jnp.sum(low * g_ref[lanes, :].astype(f32).T, axis=0, keepdims=True)
        return carry

    lax.fori_loop(0, tiles, finish, 0)

    def reduce_hop(part, d):
        return pltpu.make_async_remote_copy(
            src_ref=red_out.at[part, d], dst_ref=red_in.at[part, d - 1], send_sem=rs.at[part, d], recv_sem=rr.at[part, d - 1],
            device_id=(dp, down), device_id_type=MESH)

    def reduce_landed(part, d):
        pltpu.make_async_remote_copy(
            src_ref=red_out.at[part, d], dst_ref=red_in.at[part, d], send_sem=rs.at[part, d], recv_sem=rr.at[part, d],
            device_id=(dp, down), device_id_type=MESH).wait_recv()

    def reduce_relay(part, d):
        @pl.when(d < steps)
        def _():
            reduce_landed(part, d)

        red_out[part, d] = (sums[part, d] + red_in[part, d].astype(f32)).astype(bf16)
        reduce_hop(part, d).start()

    def back_step(n, carry):
        d = steps - n

        def tile(t, carry):
            dk, dv = carry

            @pl.when(n % 2 == 1)
            def _():
                reduce_relay(t, steps - n // 2)

            lanes = lanes_of(t)
            g, q = g_ref[lanes, :], q_ref[lanes, :]
            p = jnp.exp2(s_scr[d, :, lanes] - lse[:, lanes])
            ds = (p * (dot(kv[1, d, 0:block], g, NT) - delta[:, lanes])).astype(bf16)
            dqt[:, lanes] += dot(kt[d], ds)
            return dk + dot(ds, q), dv + dot(p.astype(bf16), g)

        zero = jnp.zeros((block, width), f32)
        sums[0, d], sums[1, d] = over_tiles(tile, (zero, zero))
        return carry

    lax.fori_loop(0, steps + 1, back_step, 0)

    def finish_dq(t, carry):
        lanes = lanes_of(t)
        dq_v[lanes, :] = (dqt[:, lanes] * scale).T.astype(bf16)
        dq_copy(t).start()
        return carry

    lax.fori_loop(0, tiles, finish_dq, 0)
    behind = (steps + 1) // 2

    def late_relay(n, carry):
        for part in range(2):
            reduce_relay(part, steps - n)
        return carry

    lax.fori_loop(behind, steps, late_relay, 0)
    ends = []
    for part, (factor, out) in enumerate(((scale, dk_out), (1.0, dv_out))):
        reduce_landed(part, 0)
        fin[part] = ((sums[part, 0] + red_in[part, 0].astype(f32)) * factor).astype(bf16)
        ends.append(send_out(fin.at[part], out, 2 * tiles + part))
        ends[-1].start()

    def drain(d, carry):
        for part in range(2):
            hop(part, d).wait_send()
            reduce_hop(part, d + 1).wait_send()
        return carry

    lax.fori_loop(0, steps, drain, 0)

    def drain_out(t, carry):
        att_copy(t).wait()
        dq_copy(t).wait()
        return carry

    lax.fori_loop(0, tiles, drain_out, 0)
    for copy in ends:
        copy.wait()


def attention(offset, heads, q, g, k, v, docs):
    rows, width = q.shape
    block = k.shape[0]
    steps = -(-DOC_MAX // block)
    window = steps + 1
    tiles = rows // ROW_TILE
    anywhere = pl.BlockSpec(memory_space=pl.ANY)
    S = jax.ShapeDtypeStruct
    dma = pltpu.SemaphoreType.DMA
    pairs = rows * block * window
    return pl.pallas_call(
        functools.partial(kernel, offset, heads, steps),
        out_shape=(S(q.shape, bf16), S(q.shape, bf16), S(k.shape, bf16), S(k.shape, bf16)),
        in_specs=[anywhere] * 5,
        out_specs=[anywhere] * 4,
        scratch_shapes=[
            pltpu.VMEM((rows, width), bf16),
            pltpu.VMEM((rows, width), bf16),
            pltpu.VMEM(docs.shape, jnp.int32),
            pltpu.VMEM((2, window, block, width), f32),
            pltpu.VMEM((2, window, block + 16, width), bf16),
            pltpu.VMEM((window, width, block), bf16),
            pltpu.VMEM((width, block), bf16),
            pltpu.VMEM((block, 128), f32),
            pltpu.VMEM((1, rows), f32),
            pltpu.VMEM((window, block, rows), f32),
            pltpu.VMEM((1, rows), f32),
            pltpu.VMEM((8, rows), f32),
            pltpu.VMEM((1, rows), f32),
            pltpu.VMEM((1, rows), f32),
            pltpu.VMEM((width, rows), f32),
            pltpu.VMEM((width, rows), f32),
            pltpu.VMEM((rows, width), bf16),
            pltpu.VMEM((rows, width), bf16),
            pltpu.VMEM((2, block, width), bf16),
            pltpu.VMEM((2, window, block, width), bf16),
            pltpu.VMEM((2, window, block, width), bf16),
            dma((2, window)), dma((2, window)), dma((2, window)), dma((2, window)),
            dma((2 * tiles + 2,)), dma((2 * tiles + 2,)), dma((5,)),
        ],
        compiler_params=pltpu.CompilerParams(collective_id=offset, has_side_effects=True, vmem_limit_bytes=56 * 2**20),
        cost_estimate=pl.CostEstimate(flops=12 * pairs * width, bytes_accessed=8 * rows * width, transcendentals=2 * pairs),
        name=f"attention_{offset}",
    )(q, g, k, v, docs)


def on_device(offsets, query, keys, values, doc_ids, grad_out, relabel):
    _, tokens, heads, width = query.shape
    flat = (query.reshape(tokens * heads, width), grad_out.reshape(tokens * heads, width), keys[0], values[0], doc_ids)
    if len(offsets) == 1:
        outs = attention(offsets[0], heads, *flat)
    else:
        outs = lax.switch(relabel[0] - 1, [functools.partial(attention, offset, heads) for offset in offsets], *flat)
    att, dq, dk, dv = outs
    return att.reshape(query.shape), dq.reshape(query.shape), dk[None], dv[None]


def solution(mesh, offsets=None):
    wide, narrow = P("dp", "ctx", None, None), P("dp", "ctx", None)
    offsets = offsets or tuple(range(1, mesh.shape["dp"]))
    return jax.shard_map(
        functools.partial(on_device, offsets), mesh=mesh,
        in_specs=(wide, narrow, narrow, P("dp", "ctx"), wide, P()),
        out_specs=(wide, wide, narrow, narrow), check_vma=False)
```
